32 devices in a mesh: head: 4 (over x, core), seq: 8 (over z, y).
Axes of the slice: x: 2, y: 2, z: 4, core: 2. Of those that a mesh axis runs over, the one named last changes fastest.
Arguments:
- tokens: bfloat16 [4, 16, 2048], P(None, None, 'seq'), may hold values from -16 to 16
- attn_in_weight: bfloat16 [3, 2048, 2048], P(None, 'seq', 'head'), may hold values from -0.125 to 0.125
- attn_out_weight: bfloat16 [2048, 2048], P('head', 'seq'), may hold values from -0.125 to 0.125
- ffn_in_weight: bfloat16 [2, 2048, 8192], P(None, 'seq', 'head'), may hold values from -0.125 to 0.125
- ffn_out_weight: bfloat16 [8192, 2048], P('head', 'seq'), may hold values from -0.0625 to 0.0625
- cache_keys: bfloat16 [16, 4096, 2048], P(None, 'seq', 'head'), may hold values from -60 to 60
- cache_values: bfloat16 [16, 4096, 2048], P(None, 'seq', 'head'), may hold values from -10 to 10
- lengths: int32 [16], replicated, may hold values from 1 to 4096, as said below
Outputs:
- attn_branch: bfloat16 [4, 16, 2048], P(None, None, 'seq')
- mlp_branch: bfloat16 [4, 16, 2048], P(None, None, 'seq')
The draws below stay inside these ranges and needn't reach their ends.
Inputs may be any that keep to these rules, and one draw needn't show every extreme that they name: `lengths`: some request has exactly 4096 filled positions.
All inputs are finite; a program needn't handle non-finite values.
Results may differ from the reference program's by a relative error of at most 0.013.
The reference program's roundings to bfloat16 on the way count: a program that leaves them out, or rounds other values in their place, can miss the bound.
Values may be sent and summed in bfloat16 or wider, within the bound.
A program may use at most 64 MiB of HBM per device.

```python
import math
import jax
import jax.numpy as jnp
from jax import lax

D = 2048
H = 16
HD = 128
FF = 8192
STEPS = 4
REQUEST_TOTAL = 16
CACHE_DEV = 512
MAX_CACHE_LENGTH = 4096


def logarithmic_uniform(key, shape, low_end, high_end):
    return jnp.exp(jax.random.uniform(key, shape, jnp.float32, math.log(low_end), math.log(high_end)))


def draw_tokens(key, part):
    key_baseline, key_rows, key_cols = jax.random.split(key, 3)
    base = jax.random.normal(key_baseline, (STEPS, REQUEST_TOTAL, D), jnp.float32)
    column = jnp.arange(D, dtype=jnp.float32) / D
    row_scale = logarithmic_uniform(key_rows, (STEPS, REQUEST_TOTAL, 1), 0.5, 2.0)
    col_scale = jnp.exp(math.log(3.0) * column) * logarithmic_uniform(key_cols, (D,), 0.6, 1.6)
    return jnp.clip(base * row_scale * col_scale, -16.0, 16.0).astype(jnp.bfloat16)


def draw_cache_keys(key, part):
    key_baseline, key_multiplier = jax.random.split(key, 2)
    base = jax.random.normal(key_baseline, (REQUEST_TOTAL, MAX_CACHE_LENGTH, H * HD), jnp.float32)
    scale_multiplier = logarithmic_uniform(key_multiplier, (REQUEST_TOTAL, MAX_CACHE_LENGTH, 1), 0.7, 2.8)
    return jnp.clip(base * scale_multiplier, -60.0, 60.0).astype(jnp.bfloat16)


def draw_cache_values(key, part):
    key_baseline, key_offset = jax.random.split(key, 2)
    base = jax.random.normal(key_baseline, (REQUEST_TOTAL, MAX_CACHE_LENGTH, H * HD), jnp.float32)
    offsets = jax.random.uniform(key_offset, (REQUEST_TOTAL, MAX_CACHE_LENGTH // 64, 1, H * HD), jnp.float32, -1.5, 1.5)
    spread_out = jnp.broadcast_to(offsets, (REQUEST_TOTAL, MAX_CACHE_LENGTH // 64, 64, H * HD)).reshape(REQUEST_TOTAL, MAX_CACHE_LENGTH, H * HD)
    return jnp.clip(base + spread_out, -10.0, 10.0).astype(jnp.bfloat16)


def draw_lengths(key, part):
    key_len, key_pick = jax.random.split(jax.random.fold_in(key, 17), 2)
    drawn = jax.random.randint(key_len, (REQUEST_TOTAL,), 1, MAX_CACHE_LENGTH + 1)
    chosen = jax.random.randint(key_pick, (), 0, REQUEST_TOTAL)
    return jnp.where(jnp.arange(REQUEST_TOTAL, dtype=jnp.int32) == chosen, MAX_CACHE_LENGTH, drawn).astype(jnp.int32)


def block_levels(stream_key, dims, pieces, least, high):
    def one(dim, parts):
        heights = jax.random.uniform(jax.random.fold_in(jax.random.fold_in(stream_key, 6), dim), (parts,), jnp.float32, least / len(pieces), high / len(pieces))
        return jnp.repeat(jnp.exp(heights), dims[dim] // parts).reshape((-1,) + (1,) * (len(dims) - dim - 1))

    gain = one(*pieces[0])
    for cut in pieces[1:]:
        gain = gain * one(*cut)
    return gain


def centred(stream_key, dims, deviation, most, cuts=(), held_as=jnp.bfloat16):
    level = block_levels(stream_key, dims, cuts, -0.22, 0.18) if cuts else 1.0
    entries = jax.random.normal(stream_key, dims, jnp.float32) * deviation * level
    return jnp.minimum(jnp.maximum(entries, -most), most).astype(held_as)


def setup_inputs(seed: int = 0) -> dict:
    streams_of = jax.random.split(jax.random.key(seed), 9)
    tokens = draw_tokens(jax.random.fold_in(streams_of[8], 71), 0)
    attn_in_weight = centred(streams_of[1], (3, D, H * HD), D ** -0.5, 0.125, ((1, 8), (2, 4)))
    attn_out_weight = centred(streams_of[2], (H * HD, D), (H * HD) ** -0.5, 0.125, ((0, 4), (1, 8)))
    ffn_in_weight = centred(streams_of[3], (2, D, FF), D ** -0.5, 0.125, ((1, 8), (2, 4)))
    ffn_out_weight = centred(streams_of[4], (FF, D), FF ** -0.5, 0.0625, ((0, 4), (1, 8)))
    cache_keys = draw_cache_keys(jax.random.fold_in(streams_of[8], 71), 0)
    cache_values = draw_cache_values(jax.random.fold_in(streams_of[8], 71), 0)
    lengths = draw_lengths(jax.random.fold_in(streams_of[8], 71), 0)
    return dict(tokens=tokens, attn_in_weight=attn_in_weight, attn_out_weight=attn_out_weight, ffn_in_weight=ffn_in_weight, ffn_out_weight=ffn_out_weight, cache_keys=cache_keys, cache_values=cache_values, lengths=lengths)


NORM_EPSILON = 1e-05
NEG_FILL = -1e+30

def layer_norm(values):
    center = lax.optimization_barrier(jnp.mean(values, axis=-1, keepdims=True))
    deviate = values - center
    spread = lax.optimization_barrier(jnp.mean(deviate * deviate, axis=-1, keepdims=True))
    return deviate * lax.rsqrt(spread + NORM_EPSILON)

def rotate_pairs(values, positions):
    half_dim = values.shape[-1] // 2
    inverse_freq = 10000.0 ** (-2.0 * jnp.arange(half_dim, dtype=jnp.float32) / values.shape[-1])
    angles = positions.astype(jnp.float32)[:, None, None] * inverse_freq[None, None, :]
    cosine = jnp.cos(angles)
    sine = jnp.sin(angles)
    first_half = values[..., :half_dim]
    second_half = values[..., half_dim:]
    return jnp.concatenate([first_half * cosine - second_half * sine, second_half * cosine + first_half * sine], axis=-1)

def reference(tokens, attn_in_weight, attn_out_weight, ffn_in_weight, ffn_out_weight, cache_keys, cache_values, lengths):
    row_count = STEPS * REQUEST_TOTAL
    inputs = tokens.reshape(row_count, D).astype(jnp.float32)
    normed = layer_norm(inputs).astype(jnp.bfloat16)
    projected = [jnp.dot(normed, attn_in_weight[index], preferred_element_type=jnp.float32) for index in range(3)]
    positions = (lengths[None, :] + jnp.arange(STEPS, dtype=jnp.int32)[:, None]).reshape(row_count)
    query = rotate_pairs(projected[0].reshape(row_count, H, HD), positions).astype(jnp.bfloat16)
    new_keys = rotate_pairs(projected[1].reshape(row_count, H, HD), positions).astype(jnp.bfloat16)
    new_values = projected[2].reshape(row_count, H, HD).astype(jnp.bfloat16)
    query = query.reshape(STEPS, REQUEST_TOTAL, H, HD).astype(jnp.float32)
    new_keys = new_keys.reshape(STEPS, REQUEST_TOTAL, H, HD).astype(jnp.float32)
    new_values = new_values.reshape(STEPS, REQUEST_TOTAL, H, HD).astype(jnp.float32)
    score_scale = 1.0 / HD ** 0.5
    block_count = MAX_CACHE_LENGTH // CACHE_DEV

    def one_block(block_index):
        first_pos = block_index * CACHE_DEV
        key_block = lax.dynamic_slice_in_dim(cache_keys, first_pos, CACHE_DEV, 1).reshape(REQUEST_TOTAL, CACHE_DEV, H, HD)
        value_block = lax.dynamic_slice_in_dim(cache_values, first_pos, CACHE_DEV, 1).reshape(REQUEST_TOTAL, CACHE_DEV, H, HD)
        scores = jnp.einsum('trhd,rchd->rthc', query, key_block.astype(jnp.float32)) * score_scale
        places = first_pos + jnp.arange(CACHE_DEV, dtype=jnp.int32)
        valid = (places[None, :] < lengths[:, None])[:, None, None, :]
        block_top = lax.optimization_barrier(jnp.max(jnp.where(valid, scores, NEG_FILL), axis=-1))
        weights = jnp.where(valid, jnp.exp(scores - block_top[..., None]), 0.0)
        block_total = lax.optimization_barrier(jnp.sum(weights, axis=-1))
        weights_bf = weights.astype(jnp.bfloat16).astype(jnp.float32)
        block_acc = jnp.einsum('rthc,rchd->rthd', weights_bf, value_block.astype(jnp.float32))
        return (block_top, block_total, block_acc)
    tops, totals, accs = lax.map(one_block, jnp.arange(block_count, dtype=jnp.int32))
    new_scores = jnp.einsum('trhd,urhd->rthu', query, new_keys) * score_scale
    causal = (jnp.arange(STEPS)[:, None] >= jnp.arange(STEPS)[None, :])[None, :, None, :]
    new_top = lax.optimization_barrier(jnp.max(jnp.where(causal, new_scores, NEG_FILL), axis=-1))
    new_weights = jnp.where(causal, jnp.exp(new_scores - new_top[..., None]), 0.0)
    new_total = lax.optimization_barrier(jnp.sum(new_weights, axis=-1))
    new_acc = jnp.einsum('rthu,urhd->rthd', new_weights.astype(jnp.bfloat16).astype(jnp.float32), new_values)
    overall = jnp.maximum(lax.optimization_barrier(jnp.max(tops, axis=0)), new_top)
    factors = jnp.exp(tops - overall[None])
    new_factor = jnp.exp(new_top - overall)
    numer = lax.optimization_barrier(jnp.sum(factors[..., None] * accs, axis=0)) + new_factor[..., None] * new_acc
    denom = lax.optimization_barrier(jnp.sum(factors * totals, axis=0)) + new_factor * new_total
    attended = (numer / denom[..., None]).transpose(1, 0, 2, 3).reshape(row_count, H * HD).astype(jnp.bfloat16)
    branch = jnp.dot(attended, attn_out_weight, preferred_element_type=jnp.float32)
    resid = inputs + branch
    normed_two = layer_norm(resid).astype(jnp.bfloat16)
    gate = jnp.dot(normed_two, ffn_in_weight[0], preferred_element_type=jnp.float32)
    upward = jnp.dot(normed_two, ffn_in_weight[1], preferred_element_type=jnp.float32)
    hidden = (jax.nn.silu(gate) * upward).astype(jnp.bfloat16)
    mlp_out = jnp.dot(hidden, ffn_out_weight, preferred_element_type=jnp.float32)
    attn_branch = branch.astype(jnp.bfloat16).reshape(STEPS, REQUEST_TOTAL, D)
    mlp_branch = mlp_out.astype(jnp.bfloat16).reshape(STEPS, REQUEST_TOTAL, D)
    return (attn_branch, mlp_branch)
```

```python
import functools

import jax
import jax.numpy as jnp
import numpy as np
from jax import lax
from jax.experimental import pallas as pl
from jax.experimental.pallas import tpu as pltpu
from jax.sharding import PartitionSpec as P

D = 2048
HD = 128
REQUESTS = 16


NORM_EPSILON = 1e-05
NEG_FILL = -1e30


def norm_rows(values):
    center = lax.psum(jnp.sum(values, axis=-1), "seq") / D
    deviate = values - center[:, None]
    spread = lax.psum(jnp.sum(deviate * deviate, axis=-1), "seq") / D
    return deviate * lax.rsqrt(spread + NORM_EPSILON)[:, None]


def rotate_pairs(values, positions):
    half_dim = values.shape[-1] // 2
    inverse_freq = 10000.0 ** (-2.0 * jnp.arange(half_dim, dtype=jnp.float32) / values.shape[-1])
    angles = positions.astype(jnp.float32)[:, None, None] * inverse_freq[None, None, :]
    cosine = jnp.cos(angles)
    sine = jnp.sin(angles)
    first_half = values[..., :half_dim]
    second_half = values[..., half_dim:]
    return jnp.concatenate(
        [first_half * cosine - second_half * sine, second_half * cosine + first_half * sine],
        axis=-1,
    )


def combine_parts(earlier, later_part):
    top_one, total_one, acc_one = earlier
    top_two, total_two, acc_two = later_part
    overall = jnp.maximum(top_one, top_two)
    factor_one = jnp.exp(top_one - overall)
    factor_two = jnp.exp(top_two - overall)
    return (
        overall,
        factor_one * total_one + factor_two * total_two,
        factor_one[..., None] * acc_one + factor_two[..., None] * acc_two,
    )


def per_device(
    tokens,
    attn_in_weight,
    attn_out_weight,
    ffn_in_weight,
    ffn_out_weight,
    cache_keys,
    cache_values,
    lengths,
):
    step_count, request_count, width_local = tokens.shape
    row_count = step_count * request_count
    inputs = tokens.reshape(row_count, width_local).astype(jnp.float32)
    normed = norm_rows(inputs).astype(jnp.bfloat16)
    partial_qkv = jnp.einsum(
        "nd,kde->kne", normed, attn_in_weight, preferred_element_type=jnp.float32
    )
    projected = lax.psum(partial_qkv, "seq")
    heads_local = attn_in_weight.shape[2] // HD
    positions = (lengths[None, :] + jnp.arange(step_count, dtype=jnp.int32)[:, None]).reshape(
        row_count
    )
    query = rotate_pairs(projected[0].reshape(row_count, heads_local, HD), positions).astype(
        jnp.bfloat16
    )
    new_keys = rotate_pairs(projected[1].reshape(row_count, heads_local, HD), positions).astype(
        jnp.bfloat16
    )
    new_values = projected[2].reshape(row_count, heads_local, HD).astype(jnp.bfloat16)
    query = query.reshape(step_count, request_count, heads_local, HD)
    new_keys = new_keys.reshape(step_count, request_count, heads_local, HD)
    new_values = new_values.reshape(step_count, request_count, heads_local, HD)
    score_scale = 1.0 / HD**0.5
    block_len = cache_keys.shape[1]
    key_block = cache_keys.reshape(request_count, block_len, heads_local, HD)
    value_block = cache_values.reshape(request_count, block_len, heads_local, HD)
    first_pos = lax.axis_index("seq") * block_len
    scores = (
        jnp.einsum("trhd,rchd->rthc", query, key_block, preferred_element_type=jnp.float32)
        * score_scale
    )
    places = first_pos + jnp.arange(block_len, dtype=jnp.int32)
    valid = (places[None, :] < lengths[:, None])[:, None, None, :]
    block_top = jnp.max(jnp.where(valid, scores, NEG_FILL), axis=-1)
    weights = jnp.where(valid, jnp.exp(scores - block_top[..., None]), 0.0)
    block_total = jnp.sum(weights, axis=-1)
    block_acc = jnp.einsum(
        "rthc,rchd->rthd",
        weights.astype(jnp.bfloat16),
        value_block,
        preferred_element_type=jnp.float32,
    )
    cache_top = lax.pmax(block_top, "seq")
    rescale = jnp.exp(block_top - cache_top)
    cache_total, cache_acc = lax.psum(
        (rescale * block_total, rescale[..., None] * block_acc), "seq"
    )
    new_scores = (
        jnp.einsum("trhd,urhd->rthu", query, new_keys, preferred_element_type=jnp.float32)
        * score_scale
    )
    causal = (jnp.arange(step_count)[:, None] >= jnp.arange(step_count)[None, :])[None, :, None, :]
    new_top = jnp.max(jnp.where(causal, new_scores, NEG_FILL), axis=-1)
    new_weights = jnp.where(causal, jnp.exp(new_scores - new_top[..., None]), 0.0)
    new_total = jnp.sum(new_weights, axis=-1)
    new_acc = jnp.einsum(
        "rthu,urhd->rthd",
        new_weights.astype(jnp.bfloat16),
        new_values,
        preferred_element_type=jnp.float32,
    )
    overall, denom, numer = combine_parts(
        (cache_top, cache_total, cache_acc), (new_top, new_total, new_acc)
    )
    attended = (
        (numer / denom[..., None])
        .transpose(1, 0, 2, 3)
        .reshape(row_count, heads_local * HD)
        .astype(jnp.bfloat16)
    )
    branch = lax.psum(
        jnp.dot(attended, attn_out_weight, preferred_element_type=jnp.float32), "head"
    )
    resid = inputs + branch
    normed_two = norm_rows(resid).astype(jnp.bfloat16)
    both = lax.psum(
        jnp.einsum("nd,kdf->knf", normed_two, ffn_in_weight, preferred_element_type=jnp.float32),
        "seq",
    )
    hidden = (jax.nn.silu(both[0]) * both[1]).astype(jnp.bfloat16)
    mlp_out = lax.psum(jnp.dot(hidden, ffn_out_weight, preferred_element_type=jnp.float32), "head")
    attn_branch = branch.astype(jnp.bfloat16).reshape(step_count, request_count, width_local)
    mlp_branch = mlp_out.astype(jnp.bfloat16).reshape(step_count, request_count, width_local)
    return (attn_branch, mlp_branch)


MESH = pl.DeviceIdType.MESH
STATS, QKV, QUERY, CACHE, ATTENDED, BRANCH, STATS_TWO, GATE_UP, HIDDEN, DOWN = range(10)
PHASES = 10


def to_row(column, eye):
    return jnp.sum(jnp.where(eye, column, 0.0), axis=0, keepdims=True)


def to_column(row, eye):
    return jnp.sum(jnp.where(eye, row, 0.0), axis=1, keepdims=True)


def layer_kernel(
    seq_count,
    head_count,
    lengths_ref,
    tokens_ref,
    freq_ref,
    win_hbm,
    wout_hbm,
    wffn_hbm,
    wdown_hbm,
    keys_hbm,
    values_hbm,
    attn_out_ref,
    mlp_out_ref,
    win,
    wout,
    wffn,
    wdown,
    keys,
    values,
    stats_buf,
    stats_two_buf,
    qkv_src,
    qkv_buf,
    query_buf,
    cache_src,
    cache_buf,
    attended_buf,
    branch_buf,
    gate_src,
    gate_buf,
    hidden_buf,
    down_buf,
    load_sem,
    keys_sem,
    values_sem,
    send_sem,
    recv_sem,
):
    me = lax.axis_index("seq")
    head_me = lax.axis_index("head")
    peers = [lax.rem(me + step, seq_count) for step in range(seq_count)]
    head_peers = [lax.rem(head_me + step, head_count) for step in range(head_count)]
    steps, requests, width = tokens_ref.shape
    rows = steps * requests
    block_len = keys.shape[1]
    cols = keys.shape[2]
    heads = cols // HD
    total_width = width * seq_count

    weight_loads = [
        pltpu.make_async_copy(source, target, load_sem.at[index])
        for index, (source, target) in enumerate(
            [(win_hbm, win), (wout_hbm, wout), (wffn_hbm, wffn), (wdown_hbm, wdown)]
        )
    ]

    def cache_load(hbm, vmem, sem, index):
        part = pl.ds(2 * index, 2)
        return pltpu.make_async_copy(hbm.at[part], vmem.at[part], sem.at[index])

    weight_loads[0].start()
    for peer in peers:
        cache_load(keys_hbm, keys, keys_sem, peer).start()
        cache_load(values_hbm, values, values_sem, peer).start()
    for load in weight_loads[1:]:
        load.start()

    barrier = pltpu.get_barrier_semaphore()
    for peer in peers[1:]:
        pl.semaphore_signal(barrier, inc=1, device_id={"seq": peer}, device_id_type=MESH)
    for peer in head_peers[1:]:
        pl.semaphore_signal(barrier, inc=1, device_id={"head": peer}, device_id_type=MESH)
    pl.semaphore_wait(barrier, seq_count + head_count - 2)

    sent = []

    def send(phase, step, source, target_buf):
        copy = pltpu.make_async_remote_copy(
            src_ref=source,
            dst_ref=target_buf.at[me],
            send_sem=send_sem.at[phase, step],
            recv_sem=recv_sem.at[phase, me],
            device_id={"seq": peers[step]},
            device_id_type=MESH,
        )
        copy.start()
        sent.append(copy)

    def arrive(phase, step, buf):
        source = lax.rem(me + seq_count - step, seq_count)
        pltpu.make_async_remote_copy(
            src_ref=buf.at[source],
            dst_ref=buf.at[source],
            send_sem=send_sem.at[phase, step],
            recv_sem=recv_sem.at[phase, source],
            device_id={"seq": peers[step]},
            device_id_type=MESH,
        ).wait_recv()
        return source

    def sum_over_heads(phase, buf, partial):
        buf[0] = partial.astype(jnp.bfloat16)
        copies = []
        for step in range(1, head_count):
            copy = pltpu.make_async_remote_copy(
                src_ref=buf.at[0],
                dst_ref=buf.at[step],
                send_sem=send_sem.at[phase, step],
                recv_sem=recv_sem.at[phase, step],
                device_id={"head": head_peers[step]},
                device_id_type=MESH,
            )
            copy.start()
            copies.append(copy)
        sent.extend(copies)
        for copy in copies:
            copy.wait_recv()
        total = jnp.zeros(partial.shape, jnp.float32)
        for device in range(head_count):
            slot = lax.rem(head_me + head_count - device, head_count)
            total = total + buf[slot].astype(jnp.float32)
        return total

    row_iota = lax.broadcasted_iota(jnp.int32, (rows, 128), 0)
    lane_iota = lax.broadcasted_iota(jnp.int32, (rows, 128), 1)
    eye = row_iota == lane_iota
    sub8 = lax.broadcasted_iota(jnp.int32, (8, 128), 0)
    lane8 = lax.broadcasted_iota(jnp.int32, (8, 128), 1)

    def normalize(values_in, phase, buf):
        center = jnp.mean(values_in, axis=1, keepdims=True)
        deviate = values_in - center
        spread = jnp.sum(deviate * deviate, axis=1, keepdims=True)
        buf[me] = jnp.where(
            sub8 == 0, to_row(center, eye), jnp.where(sub8 == 1, to_row(spread, eye), 0.0)
        )
        for step in range(1, seq_count):
            send(phase, step, buf.at[me], buf)
        for step in range(1, seq_count):
            arrive(phase, step, buf)
        slots = [buf[index] for index in range(seq_count)]
        mean = sum(slot[0:1] for slot in slots) / seq_count
        square = sum(
            slot[1:2] + width * ((slot[0:1] - mean) * (slot[0:1] - mean)) for slot in slots
        )
        scale = lax.rsqrt(square / total_width + NORM_EPSILON)
        return ((values_in - to_column(mean, eye)) * to_column(scale, eye)).astype(jnp.bfloat16)

    perm_row = lax.broadcasted_iota(jnp.int32, (rows, rows), 0)
    perm_col = lax.broadcasted_iota(jnp.int32, (rows, rows), 1)
    to_request_major = (
        (perm_row % steps) * requests + perm_row // steps == perm_col
    ).astype(jnp.bfloat16)
    to_step_major = (
        (perm_col % steps) * requests + perm_col // steps == perm_row
    ).astype(jnp.bfloat16)
    inputs = jnp.dot(
        to_request_major,
        tokens_ref[...].reshape(rows, width),
        preferred_element_type=jnp.float32,
    )
    normed = normalize(inputs, STATS, stats_buf)

    weight_loads[0].wait()
    parts = [
        jnp.dot(normed, win[index], preferred_element_type=jnp.float32) for index in range(3)
    ]
    joined = jnp.concatenate(parts, axis=1)
    half = joined.shape[1] // 2
    for index in range(seq_count):
        piece = joined[8 * index : 8 * index + 8]
        qkv_src[index] = jnp.concatenate([piece[:, :half], piece[:, half:]], axis=0).astype(
            jnp.bfloat16
        )
    for step in range(1, seq_count):
        send(QKV, step, qkv_src.at[peers[step]], qkv_buf)
    qkv_buf[me] = qkv_src[me]

    request_of = sub8 // steps
    length_rows = jnp.where(request_of == 0, lengths_ref[2 * me], lengths_ref[2 * me + 1])
    position = (length_rows + sub8 % steps).astype(jnp.float32)
    angles = position * freq_ref[...]
    cosine = jnp.cos(angles)
    sine = jnp.sin(angles)
    sine = jnp.where(lane8 < HD // 2, -sine, sine)

    for step in range(1, seq_count):
        arrive(QKV, step, qkv_buf)
    summed = sum(qkv_buf[index].astype(jnp.float32) for index in range(seq_count))
    projected = jnp.concatenate([summed[:8], summed[8:]], axis=1)

    def rotate(block):
        out = []
        for head in range(heads):
            piece = block[:, head * HD : (head + 1) * HD]
            out.append(piece * cosine + pltpu.roll(piece, HD // 2, 1) * sine)
        return jnp.concatenate(out, axis=1)

    query = rotate(projected[:, :cols])
    query_buf[me] = jnp.concatenate(
        [query[:, : cols // 2], query[:, cols // 2 :]], axis=0
    ).astype(jnp.bfloat16)
    for step in range(1, seq_count):
        send(QUERY, step, query_buf.at[me], query_buf)
    new_key = rotate(projected[:, cols : 2 * cols])
    new_value = projected[:, 2 * cols :]

    score_scale = 1.0 / HD**0.5
    lane_head = lax.broadcasted_iota(jnp.int32, (8, cols), 1) // HD
    wide_row = lax.broadcasted_iota(jnp.int32, (8 * heads, block_len), 0) % 8
    wide_place = lax.broadcasted_iota(jnp.int32, (8 * heads, block_len), 1)
    acc_row = lax.broadcasted_iota(jnp.int32, (8 * heads, cols), 0) % 8

    def spread_heads(block):
        return jnp.concatenate(
            [jnp.where(lane_head == head, block, 0.0) for head in range(heads)], axis=0
        ).astype(jnp.bfloat16)

    def unpack_query(index):
        packed = query_buf[index].astype(jnp.float32)
        return spread_heads(jnp.concatenate([packed[:8], packed[8:]], axis=1))

    def collect(top, total, acc):
        gathered = jnp.zeros((8, cols), jnp.float32)
        stats = jnp.zeros((8, 128), jnp.float32)
        for head in range(heads):
            piece = slice(8 * head, 8 * head + 8)
            gathered = jnp.where(lane_head == head, acc[piece], gathered)
            stats = jnp.where(lane8 == head, top[piece], stats)
            stats = jnp.where(lane8 == 64 + head, total[piece], stats)
        return gathered, stats

    contract_last = (((1,), (1,)), ((), ()))

    def cache_block(index):
        wide_query = unpack_query(index)
        cache_load(keys_hbm, keys, keys_sem, index).wait()
        scores = [
            lax.dot_general(
                wide_query, keys[2 * index + j], contract_last, preferred_element_type=jnp.float32
            )
            for j in range(2)
        ]
        scores = jnp.where(wide_row < steps, scores[0], scores[1]) * score_scale
        limit = jnp.where(
            wide_row < steps, lengths_ref[2 * index], lengths_ref[2 * index + 1]
        )
        valid = wide_place + me * block_len < limit
        top = jnp.max(jnp.where(valid, scores, NEG_FILL), axis=1, keepdims=True)
        weights = jnp.where(valid, jnp.exp(scores - top), 0.0)
        total = jnp.sum(weights, axis=1, keepdims=True)
        weights = weights.astype(jnp.bfloat16)
        cache_load(values_hbm, values, values_sem, index).wait()
        accs = [
            jnp.dot(weights, values[2 * index + j], preferred_element_type=jnp.float32)
            for j in range(2)
        ]
        return collect(top, total, jnp.where(acc_row < steps, accs[0], accs[1]))

    for step in range(1, seq_count):
        arrive(QUERY, step, query_buf)
    for step in list(range(1, seq_count)) + [0]:
        gathered, stats = cache_block(peers[step])
        target = cache_src.at[peers[step]] if step else cache_buf.at[me]
        target[:, :cols] = gathered
        target[:, cols:] = stats
        if step:
            send(CACHE, step, target, cache_buf)

    own_query = unpack_query(me)
    pad = jnp.zeros((120, cols), jnp.float32)
    wide_key = jnp.concatenate([new_key, pad], axis=0).astype(jnp.bfloat16)
    wide_value = jnp.concatenate([new_value, pad], axis=0).astype(jnp.bfloat16)
    new_scores = (
        lax.dot_general(own_query, wide_key, contract_last, preferred_element_type=jnp.float32)
        * score_scale
    )
    new_row = lax.broadcasted_iota(jnp.int32, new_scores.shape, 0) % 8
    new_col = lax.broadcasted_iota(jnp.int32, new_scores.shape, 1)
    causal = (
        (new_col < 8)
        & (new_col // steps == new_row // steps)
        & (new_col % steps <= new_row % steps)
    )
    new_top = jnp.max(jnp.where(causal, new_scores, NEG_FILL), axis=1, keepdims=True)
    new_weights = jnp.where(causal, jnp.exp(new_scores - new_top), 0.0)
    new_total = jnp.sum(new_weights, axis=1, keepdims=True)
    new_acc = jnp.dot(
        new_weights.astype(jnp.bfloat16), wide_value, preferred_element_type=jnp.float32
    )
    blocks = [collect(new_top, new_total, new_acc)]

    for step in range(1, seq_count):
        arrive(CACHE, step, cache_buf)
    for index in range(seq_count):
        blocks.append((cache_buf[index, :, :cols], cache_buf[index, :, cols:]))
    overall = blocks[0][1]
    for _, stats in blocks[1:]:
        overall = jnp.maximum(overall, stats)
    denom = jnp.zeros((8, 128), jnp.float32)
    numer = jnp.zeros((8, cols), jnp.float32)

    def over_lanes(block):
        return jnp.concatenate(
            [jnp.broadcast_to(block[:, head : head + 1], (8, HD)) for head in range(heads)],
            axis=1,
        )

    for acc, stats in blocks:
        factor = jnp.exp(stats - overall)
        denom = denom + factor * pltpu.roll(stats, 64, 1)
        numer = numer + over_lanes(factor) * acc
    attended = numer / over_lanes(denom)
    attended_buf[me] = jnp.concatenate(
        [attended[:, : cols // 2], attended[:, cols // 2 :]], axis=0
    ).astype(jnp.bfloat16)
    for step in range(1, seq_count):
        send(ATTENDED, step, attended_buf.at[me], attended_buf)
    weight_loads[1].wait()
    for step in range(1, seq_count):
        arrive(ATTENDED, step, attended_buf)
    packed = attended_buf[...].reshape(seq_count * 16, cols // 2)
    upper = jnp.dot(packed, wout[: cols // 2], preferred_element_type=jnp.float32)
    lower = jnp.dot(packed, wout[cols // 2 :], preferred_element_type=jnp.float32)
    partial = (
        upper.reshape(seq_count, 16, width)[:, :8] + lower.reshape(seq_count, 16, width)[:, 8:]
    ).reshape(rows, width)
    branch = sum_over_heads(BRANCH, branch_buf, partial)

    def put_out(ref, value):
        ref[...] = (
            jnp.dot(to_step_major, value.astype(jnp.bfloat16), preferred_element_type=jnp.float32)
            .astype(jnp.bfloat16)
            .reshape(ref.shape)
        )

    put_out(attn_out_ref, branch)
    normed_two = normalize(inputs + branch, STATS_TWO, stats_two_buf)

    weight_loads[2].wait()
    part = wffn.shape[2] // seq_count
    for step in list(range(1, seq_count)) + [0]:
        place = pl.ds(pl.multiple_of(peers[step] * part, part), part)
        target = gate_src.at[peers[step]] if step else gate_buf.at[me]
        for index in range(2):
            target[:, index * part : (index + 1) * part] = jnp.dot(
                normed_two, wffn[index, :, place], preferred_element_type=jnp.float32
            ).astype(jnp.bfloat16)
        if step:
            send(GATE_UP, step, target, gate_buf)
    for step in range(1, seq_count):
        arrive(GATE_UP, step, gate_buf)
    both = sum(gate_buf[index].astype(jnp.float32) for index in range(seq_count))
    gate = both[:, :part]
    hidden_buf[me] = (gate / (1.0 + jnp.exp(-gate)) * both[:, part:]).astype(jnp.bfloat16)
    for step in range(1, seq_count):
        send(HIDDEN, step, hidden_buf.at[me], hidden_buf)
    weight_loads[3].wait()
    partial = jnp.zeros((rows, width), jnp.float32)
    for step in range(seq_count):
        source = arrive(HIDDEN, step, hidden_buf) if step else me
        place = pl.ds(pl.multiple_of(source * part, part), part)
        partial = partial + jnp.dot(
            hidden_buf[source], wdown[place, :], preferred_element_type=jnp.float32
        )
    put_out(mlp_out_ref, sum_over_heads(DOWN, down_buf, partial))
    for copy in sent:
        copy.wait_send()


def fused_device(
    tokens,
    attn_in_weight,
    attn_out_weight,
    ffn_in_weight,
    ffn_out_weight,
    cache_keys,
    cache_values,
    lengths,
    *,
    seq_count,
    head_count,
):
    rows = tokens.shape[0] * tokens.shape[1]
    width = tokens.shape[2]
    cols = cache_keys.shape[2]
    part = ffn_in_weight.shape[2] // seq_count
    inverse_freq = 10000.0 ** (-2.0 * np.arange(HD // 2) / HD)
    freq = jnp.asarray(np.tile(inverse_freq, 2)[None, :].astype(np.float32))
    bf16, f32 = jnp.bfloat16, jnp.float32
    in_vmem = pl.BlockSpec(memory_space=pltpu.VMEM)
    in_any = pl.BlockSpec(memory_space=pl.ANY)
    weights = (attn_in_weight, attn_out_weight, ffn_in_weight, ffn_out_weight)
    caches = (cache_keys, cache_values)
    return pl.pallas_call(
        functools.partial(layer_kernel, seq_count, head_count),
        out_shape=[jax.ShapeDtypeStruct(tokens.shape, bf16)] * 2,
        in_specs=[pl.BlockSpec(memory_space=pltpu.SMEM), in_vmem, in_vmem] + [in_any] * 6,
        out_specs=[in_vmem] * 2,
        scratch_shapes=[pltpu.VMEM(array.shape, bf16) for array in weights + caches]
        + [
            pltpu.VMEM((seq_count, 8, 128), f32),
            pltpu.VMEM((seq_count, 8, 128), f32),
            pltpu.VMEM((seq_count, 16, 3 * cols // 2), bf16),
            pltpu.VMEM((seq_count, 16, 3 * cols // 2), bf16),
            pltpu.VMEM((seq_count, 16, cols // 2), bf16),
            pltpu.VMEM((seq_count, 8, cols + 128), f32),
            pltpu.VMEM((seq_count, 8, cols + 128), f32),
            pltpu.VMEM((seq_count, 16, cols // 2), bf16),
            pltpu.VMEM((head_count, rows, width), bf16),
            pltpu.VMEM((seq_count, rows, 2 * part), bf16),
            pltpu.VMEM((seq_count, rows, 2 * part), bf16),
            pltpu.VMEM((seq_count, rows, part), bf16),
            pltpu.VMEM((head_count, rows, width), bf16),
            pltpu.SemaphoreType.DMA((4,)),
            pltpu.SemaphoreType.DMA((seq_count,)),
            pltpu.SemaphoreType.DMA((seq_count,)),
            pltpu.SemaphoreType.DMA((PHASES, max(seq_count, head_count))),
            pltpu.SemaphoreType.DMA((PHASES, max(seq_count, head_count))),
        ],
        compiler_params=pltpu.CompilerParams(
            collective_id=0, has_side_effects=True, vmem_limit_bytes=48 * 2**20
        ),
        cost_estimate=pl.CostEstimate(
            flops=2 * rows * width * (attn_in_weight.size + ffn_in_weight.size) // width,
            bytes_accessed=2 * sum(array.size for array in weights + caches),
            transcendentals=0,
        ),
    )(lengths, tokens, freq, *weights, *caches)


def fits_fused(mesh):
    seq_count, head_count = mesh.shape["seq"], mesh.shape["head"]
    return REQUESTS == 2 * seq_count and D % (128 * seq_count) == 0 and D % (256 * head_count) == 0


def solution(mesh):
    in_specs = (
        P(None, None, "seq"),
        P(None, "seq", "head"),
        P("head", "seq"),
        P(None, "seq", "head"),
        P("head", "seq"),
        P(None, "seq", "head"),
        P(None, "seq", "head"),
        P(),
    )
    out_specs = (P(None, None, "seq"), P(None, None, "seq"))
    body = per_device
    if fits_fused(mesh):
        body = functools.partial(
            fused_device, seq_count=mesh.shape["seq"], head_count=mesh.shape["head"]
        )
    return jax.shard_map(
        body, mesh=mesh, in_specs=in_specs, out_specs=out_specs, check_vma=False
    )
```

```python
import functools

import jax
import jax.numpy as jnp
import numpy as np
from jax import lax
from jax.experimental import pallas as pl
from jax.experimental.pallas import tpu as pltpu
from jax.sharding import PartitionSpec as P

D = 2048
HD = 128
REQUESTS = 16


NORM_EPSILON = 1e-05
NEG_FILL = -1e30


def norm_rows(values):
    center = lax.psum(jnp.sum(values, axis=-1), "seq") / D
    deviate = values - center[:, None]
    spread = lax.psum(jnp.sum(deviate * deviate, axis=-1), "seq") / D
    return deviate * lax.rsqrt(spread + NORM_EPSILON)[:, None]


def rotate_pairs(values, positions):
    half_dim = values.shape[-1] // 2
    inverse_freq = 10000.0 ** (-2.0 * jnp.arange(half_dim, dtype=jnp.float32) / values.shape[-1])
    angles = positions.astype(jnp.float32)[:, None, None] * inverse_freq[None, None, :]
    cosine = jnp.cos(angles)
    sine = jnp.sin(angles)
    first_half = values[..., :half_dim]
    second_half = values[..., half_dim:]
    return jnp.concatenate(
        [first_half * cosine - second_half * sine, second_half * cosine + first_half * sine],
        axis=-1,
    )


def combine_parts(earlier, later_part):
    top_one, total_one, acc_one = earlier
    top_two, total_two, acc_two = later_part
    overall = jnp.maximum(top_one, top_two)
    factor_one = jnp.exp(top_one - overall)
    factor_two = jnp.exp(top_two - overall)
    return (
        overall,
        factor_one * total_one + factor_two * total_two,
        factor_one[..., None] * acc_one + factor_two[..., None] * acc_two,
    )


def per_device(
    tokens,
    attn_in_weight,
    attn_out_weight,
    ffn_in_weight,
    ffn_out_weight,
    cache_keys,
    cache_values,
    lengths,
):
    step_count, request_count, width_local = tokens.shape
    row_count = step_count * request_count
    inputs = tokens.reshape(row_count, width_local).astype(jnp.float32)
    normed = norm_rows(inputs).astype(jnp.bfloat16)
    partial_qkv = jnp.einsum(
        "nd,kde->kne", normed, attn_in_weight, preferred_element_type=jnp.float32
    )
    projected = lax.psum(partial_qkv, "seq")
    heads_local = attn_in_weight.shape[2] // HD
    positions = (lengths[None, :] + jnp.arange(step_count, dtype=jnp.int32)[:, None]).reshape(
        row_count
    )
    query = rotate_pairs(projected[0].reshape(row_count, heads_local, HD), positions).astype(
        jnp.bfloat16
    )
    new_keys = rotate_pairs(projected[1].reshape(row_count, heads_local, HD), positions).astype(
        jnp.bfloat16
    )
    new_values = projected[2].reshape(row_count, heads_local, HD).astype(jnp.bfloat16)
    query = query.reshape(step_count, request_count, heads_local, HD)
    new_keys = new_keys.reshape(step_count, request_count, heads_local, HD)
    new_values = new_values.reshape(step_count, request_count, heads_local, HD)
    score_scale = 1.0 / HD**0.5
    block_len = cache_keys.shape[1]
    key_block = cache_keys.reshape(request_count, block_len, heads_local, HD)
    value_block = cache_values.reshape(request_count, block_len, heads_local, HD)
    first_pos = lax.axis_index("seq") * block_len
    scores = (
        jnp.einsum("trhd,rchd->rthc", query, key_block, preferred_element_type=jnp.float32)
        * score_scale
    )
    places = first_pos + jnp.arange(block_len, dtype=jnp.int32)
    valid = (places[None, :] < lengths[:, None])[:, None, None, :]
    block_top = jnp.max(jnp.where(valid, scores, NEG_FILL), axis=-1)
    weights = jnp.where(valid, jnp.exp(scores - block_top[..., None]), 0.0)
    block_total = jnp.sum(weights, axis=-1)
    block_acc = jnp.einsum(
        "rthc,rchd->rthd",
        weights.astype(jnp.bfloat16),
        value_block,
        preferred_element_type=jnp.float32,
    )
    cache_top = lax.pmax(block_top, "seq")
    rescale = jnp.exp(block_top - cache_top)
    cache_total, cache_acc = lax.psum(
        (rescale * block_total, rescale[..., None] * block_acc), "seq"
    )
    new_scores = (
        jnp.einsum("trhd,urhd->rthu", query, new_keys, preferred_element_type=jnp.float32)
        * score_scale
    )
    causal = (jnp.arange(step_count)[:, None] >= jnp.arange(step_count)[None, :])[None, :, None, :]
    new_top = jnp.max(jnp.where(causal, new_scores, NEG_FILL), axis=-1)
    new_weights = jnp.where(causal, jnp.exp(new_scores - new_top[..., None]), 0.0)
    new_total = jnp.sum(new_weights, axis=-1)
    new_acc = jnp.einsum(
        "rthu,urhd->rthd",
        new_weights.astype(jnp.bfloat16),
        new_values,
        preferred_element_type=jnp.float32,
    )
    overall, denom, numer = combine_parts(
        (cache_top, cache_total, cache_acc), (new_top, new_total, new_acc)
    )
    attended = (
        (numer / denom[..., None])
        .transpose(1, 0, 2, 3)
        .reshape(row_count, heads_local * HD)
        .astype(jnp.bfloat16)
    )
    branch = lax.psum(
        jnp.dot(attended, attn_out_weight, preferred_element_type=jnp.float32), "head"
    )
    resid = inputs + branch
    normed_two = norm_rows(resid).astype(jnp.bfloat16)
    both = lax.psum(
        jnp.einsum("nd,kdf->knf", normed_two, ffn_in_weight, preferred_element_type=jnp.float32),
        "seq",
    )
    hidden = (jax.nn.silu(both[0]) * both[1]).astype(jnp.bfloat16)
    mlp_out = lax.psum(jnp.dot(hidden, ffn_out_weight, preferred_element_type=jnp.float32), "head")
    attn_branch = branch.astype(jnp.bfloat16).reshape(step_count, request_count, width_local)
    mlp_branch = mlp_out.astype(jnp.bfloat16).reshape(step_count, request_count, width_local)
    return (attn_branch, mlp_branch)


MESH = pl.DeviceIdType.MESH
(
    STATS, QKV, QUERY, CACHE, ATTENDED, BRANCH, STATS_TWO, GATE_UP, HIDDEN, DOWN,
    COLUMN_SUM, GATE_UP_PAIR, HIDDEN_PAIR,
) = range(13)
PHASES = 13
PAIR = 2


def to_row(column, eye):
    return jnp.sum(jnp.where(eye, column, 0.0), axis=0, keepdims=True)


def to_column(row, eye):
    return jnp.sum(jnp.where(eye, row, 0.0), axis=1, keepdims=True)


def layer_kernel(
    seq_count,
    head_count,
    lengths_ref,
    tokens_ref,
    freq_ref,
    win_hbm,
    wout_hbm,
    wffn_hbm,
    wdown_hbm,
    keys_hbm,
    values_hbm,
    attn_out_ref,
    mlp_out_ref,
    win,
    wout,
    wffn,
    wdown,
    keys,
    values,
    stats_buf,
    stats_two_buf,
    qkv_src,
    qkv_buf,
    query_buf,
    cache_src,
    cache_buf,
    attended_buf,
    branch_buf,
    column_src,
    column_buf,
    pair_src,
    pair_buf,
    line_src,
    line_buf,
    hidden_buf,
    down_buf,
    load_sem,
    keys_sem,
    values_sem,
    send_sem,
    recv_sem,
):
    me = lax.axis_index("seq")
    head_me = lax.axis_index("head")
    peers = [lax.rem(me + step, seq_count) for step in range(seq_count)]
    head_peers = [lax.rem(head_me + step, head_count) for step in range(head_count)]
    steps, requests, width = tokens_ref.shape
    rows = steps * requests
    block_len = keys.shape[1]
    cols = keys.shape[2]
    heads = cols // HD
    total_width = width * seq_count

    weight_loads = [
        pltpu.make_async_copy(source, target, load_sem.at[index])
        for index, (source, target) in enumerate(
            [(win_hbm, win), (wout_hbm, wout), (wffn_hbm, wffn), (wdown_hbm, wdown)]
        )
    ]

    def cache_load(hbm, vmem, sem, index):
        part = pl.ds(2 * index, 2)
        return pltpu.make_async_copy(hbm.at[part], vmem.at[part], sem.at[index])

    weight_loads[0].start()
    for peer in peers:
        cache_load(keys_hbm, keys, keys_sem, peer).start()
        cache_load(values_hbm, values, values_sem, peer).start()
    for load in weight_loads[1:]:
        load.start()

    barrier = pltpu.get_barrier_semaphore()
    for peer in peers[1:]:
        pl.semaphore_signal(barrier, inc=1, device_id={"seq": peer}, device_id_type=MESH)
    for peer in head_peers[1:]:
        pl.semaphore_signal(barrier, inc=1, device_id={"head": peer}, device_id_type=MESH)
    pl.semaphore_wait(barrier, seq_count + head_count - 2)

    sent = []

    def push(source, target, send_slot, recv_slot, peer):
        copy = pltpu.make_async_remote_copy(
            src_ref=source,
            dst_ref=target,
            send_sem=send_sem.at[send_slot[0], send_slot[1]],
            recv_sem=recv_sem.at[recv_slot[0], recv_slot[1]],
            device_id={"seq": peer},
            device_id_type=MESH,
        )
        copy.start()
        sent.append(copy)

    def landed(buf, recv_slot):
        pltpu.make_async_remote_copy(
            src_ref=buf,
            dst_ref=buf,
            send_sem=send_sem.at[recv_slot[0], 0],
            recv_sem=recv_sem.at[recv_slot[0], recv_slot[1]],
            device_id={"seq": peers[1]},
            device_id_type=MESH,
        ).wait_recv()

    def send(phase, step, source, target_buf):
        copy = pltpu.make_async_remote_copy(
            src_ref=source,
            dst_ref=target_buf.at[me],
            send_sem=send_sem.at[phase, step],
            recv_sem=recv_sem.at[phase, me],
            device_id={"seq": peers[step]},
            device_id_type=MESH,
        )
        copy.start()
        sent.append(copy)

    def arrive(phase, step, buf):
        source = lax.rem(me + seq_count - step, seq_count)
        pltpu.make_async_remote_copy(
            src_ref=buf.at[source],
            dst_ref=buf.at[source],
            send_sem=send_sem.at[phase, step],
            recv_sem=recv_sem.at[phase, source],
            device_id={"seq": peers[step]},
            device_id_type=MESH,
        ).wait_recv()
        return source

    def sum_over_heads(phase, buf, partial):
        buf[0] = partial.astype(jnp.bfloat16)
        copies = []
        for step in range(1, head_count):
            copy = pltpu.make_async_remote_copy(
                src_ref=buf.at[0],
                dst_ref=buf.at[step],
                send_sem=send_sem.at[phase, step],
                recv_sem=recv_sem.at[phase, step],
                device_id={"head": head_peers[step]},
                device_id_type=MESH,
            )
            copy.start()
            copies.append(copy)
        sent.extend(copies)
        for copy in copies:
            copy.wait_recv()
        total = jnp.zeros(partial.shape, jnp.float32)
        for device in range(head_count):
            slot = lax.rem(head_me + head_count - device, head_count)
            total = total + buf[slot].astype(jnp.float32)
        return total

    row_iota = lax.broadcasted_iota(jnp.int32, (rows, 128), 0)
    lane_iota = lax.broadcasted_iota(jnp.int32, (rows, 128), 1)
    eye = row_iota == lane_iota
    sub8 = lax.broadcasted_iota(jnp.int32, (8, 128), 0)
    lane8 = lax.broadcasted_iota(jnp.int32, (8, 128), 1)

    def send_stats(values_in, phase, buf):
        center = jnp.mean(values_in, axis=1, keepdims=True)
        deviate = values_in - center
        spread = jnp.sum(deviate * deviate, axis=1, keepdims=True)
        buf[me] = jnp.where(
            sub8 == 0, to_row(center, eye), jnp.where(sub8 == 1, to_row(spread, eye), 0.0)
        )
        for step in range(1, seq_count):
            send(phase, step, buf.at[me], buf)
        return deviate

    def join_stats(phase, buf):
        for step in range(1, seq_count):
            arrive(phase, step, buf)
        slots = [buf[index] for index in range(seq_count)]
        mean = sum(slot[0:1] for slot in slots) / seq_count
        offsets = [slot[0:1] - mean for slot in slots]
        square = sum(
            slot[1:2] + width * (offset * offset) for slot, offset in zip(slots, offsets)
        )
        return mean, offsets, lax.rsqrt(square / total_width + NORM_EPSILON)

    perm_row = lax.broadcasted_iota(jnp.int32, (rows, rows), 0)
    perm_col = lax.broadcasted_iota(jnp.int32, (rows, rows), 1)
    to_request_major = (
        (perm_row % steps) * requests + perm_row // steps == perm_col
    ).astype(jnp.bfloat16)
    to_step_major = (
        (perm_col % steps) * requests + perm_col // steps == perm_row
    ).astype(jnp.bfloat16)
    inputs = jnp.dot(
        to_request_major,
        tokens_ref[...].reshape(rows, width),
        preferred_element_type=jnp.float32,
    )
    send_stats(inputs, STATS, stats_buf)
    mean, _, scale = join_stats(STATS, stats_buf)
    normed = ((inputs - to_column(mean, eye)) * to_column(scale, eye)).astype(jnp.bfloat16)

    weight_loads[0].wait()
    parts = [
        jnp.dot(normed, win[index], preferred_element_type=jnp.float32) for index in range(3)
    ]
    joined = jnp.concatenate(parts, axis=1)
    half = joined.shape[1] // 2
    for index in range(seq_count):
        piece = joined[8 * index : 8 * index + 8]
        qkv_src[index] = jnp.concatenate([piece[:, :half], piece[:, half:]], axis=0).astype(
            jnp.bfloat16
        )
    for step in range(1, seq_count):
        send(QKV, step, qkv_src.at[peers[step]], qkv_buf)
    qkv_buf[me] = qkv_src[me]

    request_of = sub8 // steps
    length_rows = jnp.where(request_of == 0, lengths_ref[2 * me], lengths_ref[2 * me + 1])
    position = (length_rows + sub8 % steps).astype(jnp.float32)
    angles = position * freq_ref[...]
    cosine = jnp.cos(angles)
    sine = jnp.sin(angles)
    sine = jnp.where(lane8 < HD // 2, -sine, sine)

    for step in range(1, seq_count):
        arrive(QKV, step, qkv_buf)
    summed = sum(qkv_buf[index].astype(jnp.float32) for index in range(seq_count))
    projected = jnp.concatenate([summed[:8], summed[8:]], axis=1)

    def rotate(block):
        out = []
        for head in range(heads):
            piece = block[:, head * HD : (head + 1) * HD]
            out.append(piece * cosine + pltpu.roll(piece, HD // 2, 1) * sine)
        return jnp.concatenate(out, axis=1)

    query = rotate(projected[:, :cols])
    query_buf[me] = jnp.concatenate(
        [query[:, : cols // 2], query[:, cols // 2 :]], axis=0
    ).astype(jnp.bfloat16)
    for step in range(1, seq_count):
        send(QUERY, step, query_buf.at[me], query_buf)
    new_key = rotate(projected[:, cols : 2 * cols])
    new_value = projected[:, 2 * cols :]

    part = wffn.shape[2] // seq_count
    weight_loads[2].wait()
    ones = jnp.ones((16, width), jnp.bfloat16)
    column_sums = [
        jnp.dot(ones, wffn[index], preferred_element_type=jnp.float32)[:8] for index in range(2)
    ]
    pieces = part // 128
    for index in range(seq_count):
        packed = jnp.zeros((8, 128), jnp.float32)
        for piece in range(2 * pieces):
            start = index * part + (piece % pieces) * 128
            packed = jnp.where(
                sub8 == piece, column_sums[piece // pieces][:, start : start + 128], packed
            )
        column_src[index] = packed
    column_buf[me] = column_src[me]
    for step in range(1, seq_count):
        send(COLUMN_SUM, step, column_src.at[peers[step]], column_buf)

    score_scale = 1.0 / HD**0.5
    lane_head = lax.broadcasted_iota(jnp.int32, (8, cols), 1) // HD
    wide_row = lax.broadcasted_iota(jnp.int32, (8 * heads, block_len), 0) % 8
    wide_place = lax.broadcasted_iota(jnp.int32, (8 * heads, block_len), 1)
    acc_row = lax.broadcasted_iota(jnp.int32, (8 * heads, cols), 0) % 8

    def spread_heads(block):
        return jnp.concatenate(
            [jnp.where(lane_head == head, block, 0.0) for head in range(heads)], axis=0
        ).astype(jnp.bfloat16)

    def unpack_query(index):
        packed = query_buf[index].astype(jnp.float32)
        return spread_heads(jnp.concatenate([packed[:8], packed[8:]], axis=1))

    def collect(top, total, acc):
        gathered = jnp.zeros((8, cols), jnp.float32)
        stats = jnp.zeros((8, 128), jnp.float32)
        for head in range(heads):
            piece = slice(8 * head, 8 * head + 8)
            gathered = jnp.where(lane_head == head, acc[piece], gathered)
            stats = jnp.where(lane8 == head, top[piece], stats)
            stats = jnp.where(lane8 == 64 + head, total[piece], stats)
        return gathered, stats

    contract_last = (((1,), (1,)), ((), ()))

    def cache_block(index):
        wide_query = unpack_query(index)
        cache_load(keys_hbm, keys, keys_sem, index).wait()
        scores = [
            lax.dot_general(
                wide_query, keys[2 * index + j], contract_last, preferred_element_type=jnp.float32
            )
            for j in range(2)
        ]
        scores = jnp.where(wide_row < steps, scores[0], scores[1]) * score_scale
        limit = jnp.where(
            wide_row < steps, lengths_ref[2 * index], lengths_ref[2 * index + 1]
        )
        valid = wide_place + me * block_len < limit
        top = jnp.max(jnp.where(valid, scores, NEG_FILL), axis=1, keepdims=True)
        weights = jnp.where(valid, jnp.exp(scores - top), 0.0)
        total = jnp.sum(weights, axis=1, keepdims=True)
        weights = weights.astype(jnp.bfloat16)
        cache_load(values_hbm, values, values_sem, index).wait()
        accs = [
            jnp.dot(weights, values[2 * index + j], preferred_element_type=jnp.float32)
            for j in range(2)
        ]
        return collect(top, total, jnp.where(acc_row < steps, accs[0], accs[1]))

    for step in range(1, seq_count):
        arrive(QUERY, step, query_buf)
    for step in list(range(1, seq_count)) + [0]:
        gathered, stats = cache_block(peers[step])
        target = cache_src.at[peers[step]] if step else cache_buf.at[me]
        target[:, :cols] = gathered
        target[:, cols:] = stats
        if step:
            send(CACHE, step, target, cache_buf)

    own_query = unpack_query(me)
    pad = jnp.zeros((120, cols), jnp.float32)
    wide_key = jnp.concatenate([new_key, pad], axis=0).astype(jnp.bfloat16)
    wide_value = jnp.concatenate([new_value, pad], axis=0).astype(jnp.bfloat16)
    new_scores = (
        lax.dot_general(own_query, wide_key, contract_last, preferred_element_type=jnp.float32)
        * score_scale
    )
    new_row = lax.broadcasted_iota(jnp.int32, new_scores.shape, 0) % 8
    new_col = lax.broadcasted_iota(jnp.int32, new_scores.shape, 1)
    causal = (
        (new_col < 8)
        & (new_col // steps == new_row // steps)
        & (new_col % steps <= new_row % steps)
    )
    new_top = jnp.max(jnp.where(causal, new_scores, NEG_FILL), axis=1, keepdims=True)
    new_weights = jnp.where(causal, jnp.exp(new_scores - new_top), 0.0)
    new_total = jnp.sum(new_weights, axis=1, keepdims=True)
    new_acc = jnp.dot(
        new_weights.astype(jnp.bfloat16), wide_value, preferred_element_type=jnp.float32
    )
    blocks = [collect(new_top, new_total, new_acc)]

    for step in range(1, seq_count):
        arrive(CACHE, step, cache_buf)
    for index in range(seq_count):
        blocks.append((cache_buf[index, :, :cols], cache_buf[index, :, cols:]))
    overall = blocks[0][1]
    for _, stats in blocks[1:]:
        overall = jnp.maximum(overall, stats)
    denom = jnp.zeros((8, 128), jnp.float32)
    numer = jnp.zeros((8, cols), jnp.float32)

    def over_lanes(block):
        return jnp.concatenate(
            [jnp.broadcast_to(block[:, head : head + 1], (8, HD)) for head in range(heads)],
            axis=1,
        )

    for acc, stats in blocks:
        factor = jnp.exp(stats - overall)
        denom = denom + factor * pltpu.roll(stats, 64, 1)
        numer = numer + over_lanes(factor) * acc
    attended = numer / over_lanes(denom)
    attended_buf[me] = jnp.concatenate(
        [attended[:, : cols // 2], attended[:, cols // 2 :]], axis=0
    ).astype(jnp.bfloat16)
    for step in range(1, seq_count):
        send(ATTENDED, step, attended_buf.at[me], attended_buf)
    weight_loads[1].wait()
    for step in range(1, seq_count):
        arrive(ATTENDED, step, attended_buf)
    packed = attended_buf[...].reshape(seq_count * 16, cols // 2)
    upper = jnp.dot(packed, wout[: cols // 2], preferred_element_type=jnp.float32)
    lower = jnp.dot(packed, wout[cols // 2 :], preferred_element_type=jnp.float32)
    partial = (
        upper.reshape(seq_count, 16, width)[:, :8] + lower.reshape(seq_count, 16, width)[:, 8:]
    ).reshape(rows, width)
    branch = sum_over_heads(BRANCH, branch_buf, partial)

    def put_out(ref, value):
        ref[...] = (
            jnp.dot(to_step_major, value.astype(jnp.bfloat16), preferred_element_type=jnp.float32)
            .astype(jnp.bfloat16)
            .reshape(ref.shape)
        )

    put_out(attn_out_ref, branch)
    lines = seq_count // PAIR
    line, place_in_pair = me // PAIR, me % PAIR
    partner = line * PAIR + (PAIR - 1 - place_in_pair)
    line_peers = [lax.rem(line + step, lines) * PAIR + place_in_pair for step in range(lines)]
    across = [lax.rem(line + step, lines) * PAIR + (PAIR - 1 - place_in_pair) for step in range(lines)]
    centred = send_stats(inputs + branch, STATS_TWO, stats_two_buf).astype(jnp.bfloat16)

    def gate_up(index):
        place = pl.ds(pl.multiple_of(index * part, part), part)
        return jnp.concatenate(
            [
                jnp.dot(centred, wffn[which, :, place], preferred_element_type=jnp.float32)
                for which in range(2)
            ],
            axis=1,
        )

    order = list(range(1, lines)) + [0]
    for step in order:
        pair_src[step] = gate_up(across[step]).astype(jnp.bfloat16)
        push(
            pair_src.at[step], pair_buf.at[step], (GATE_UP_PAIR, step), (GATE_UP_PAIR, step), partner
        )
    for step in order:
        own = gate_up(line_peers[step])
        landed(pair_buf.at[step], (GATE_UP_PAIR, step))
        both = own + pair_buf[step].astype(jnp.float32)
        if step:
            line_src[step] = both.astype(jnp.bfloat16)
            push(
                line_src.at[step],
                line_buf.at[step],
                (GATE_UP, step),
                (GATE_UP, step),
                line_peers[step],
            )
    _, offsets, scale = join_stats(STATS_TWO, stats_two_buf)
    for step in range(1, seq_count):
        arrive(COLUMN_SUM, step, column_buf)
    for index in range(seq_count):
        sums = column_buf[index]
        sums = jnp.concatenate([sums[j : j + 1] for j in range(2 * pieces)], axis=1)
        both = both + to_column(offsets[index], eye) * sums
    scale = to_column(scale, eye)
    for step in range(1, lines):
        landed(line_buf.at[step], (GATE_UP, step))
        both = both + line_buf[step].astype(jnp.float32)
    both = both * scale
    gate = both[:, :part]
    hidden_buf[me] = (gate / (1.0 + jnp.exp(-gate)) * both[:, part:]).astype(jnp.bfloat16)

    def share(index, step):
        push(
            hidden_buf.at[index], hidden_buf.at[index], (HIDDEN_PAIR, step), (HIDDEN, index), partner
        )

    def down(index):
        place = pl.ds(pl.multiple_of(index * part, part), part)
        return jnp.dot(hidden_buf[index], wdown[place, :], preferred_element_type=jnp.float32)

    for step in range(1, lines):
        push(hidden_buf.at[me], hidden_buf.at[me], (HIDDEN, step), (HIDDEN, me), line_peers[step])
    share(me, 0)
    weight_loads[3].wait()
    partial = down(me)
    for step in range(1, lines):
        landed(hidden_buf.at[line_peers[step]], (HIDDEN, line_peers[step]))
        share(line_peers[step], step)
        partial = partial + down(line_peers[step])
    for step in range(lines):
        landed(hidden_buf.at[across[step]], (HIDDEN, across[step]))
        partial = partial + down(across[step])
    put_out(mlp_out_ref, sum_over_heads(DOWN, down_buf, partial))
    for copy in sent:
        copy.wait_send()


def fused_device(
    tokens,
    attn_in_weight,
    attn_out_weight,
    ffn_in_weight,
    ffn_out_weight,
    cache_keys,
    cache_values,
    lengths,
    *,
    seq_count,
    head_count,
):
    rows = tokens.shape[0] * tokens.shape[1]
    width = tokens.shape[2]
    cols = cache_keys.shape[2]
    part = ffn_in_weight.shape[2] // seq_count
    inverse_freq = 10000.0 ** (-2.0 * np.arange(HD // 2) / HD)
    freq = jnp.asarray(np.tile(inverse_freq, 2)[None, :].astype(np.float32))
    bf16, f32 = jnp.bfloat16, jnp.float32
    in_vmem = pl.BlockSpec(memory_space=pltpu.VMEM)
    in_any = pl.BlockSpec(memory_space=pl.ANY)
    weights = (attn_in_weight, attn_out_weight, ffn_in_weight, ffn_out_weight)
    caches = (cache_keys, cache_values)
    return pl.pallas_call(
        functools.partial(layer_kernel, seq_count, head_count),
        out_shape=[jax.ShapeDtypeStruct(tokens.shape, bf16)] * 2,
        in_specs=[pl.BlockSpec(memory_space=pltpu.SMEM), in_vmem, in_vmem] + [in_any] * 6,
        out_specs=[in_vmem] * 2,
        scratch_shapes=[pltpu.VMEM(array.shape, bf16) for array in weights + caches]
        + [
            pltpu.VMEM((seq_count, 8, 128), f32),
            pltpu.VMEM((seq_count, 8, 128), f32),
            pltpu.VMEM((seq_count, 16, 3 * cols // 2), bf16),
            pltpu.VMEM((seq_count, 16, 3 * cols // 2), bf16),
            pltpu.VMEM((seq_count, 16, cols // 2), bf16),
            pltpu.VMEM((seq_count, 8, cols + 128), f32),
            pltpu.VMEM((seq_count, 8, cols + 128), f32),
            pltpu.VMEM((seq_count, 16, cols // 2), bf16),
            pltpu.VMEM((head_count, rows, width), bf16),
            pltpu.VMEM((seq_count, 8, 128), f32),
            pltpu.VMEM((seq_count, 8, 128), f32),
            pltpu.VMEM((seq_count // PAIR, rows, 2 * part), bf16),
            pltpu.VMEM((seq_count // PAIR, rows, 2 * part), bf16),
            pltpu.VMEM((seq_count // PAIR, rows, 2 * part), bf16),
            pltpu.VMEM((seq_count // PAIR, rows, 2 * part), bf16),
            pltpu.VMEM((seq_count, rows, part), bf16),
            pltpu.VMEM((head_count, rows, width), bf16),
            pltpu.SemaphoreType.DMA((4,)),
            pltpu.SemaphoreType.DMA((seq_count,)),
            pltpu.SemaphoreType.DMA((seq_count,)),
            pltpu.SemaphoreType.DMA((PHASES, max(seq_count, head_count))),
            pltpu.SemaphoreType.DMA((PHASES, max(seq_count, head_count))),
        ],
        compiler_params=pltpu.CompilerParams(
            collective_id=0, has_side_effects=True, vmem_limit_bytes=60 * 2**20
        ),
        cost_estimate=pl.CostEstimate(
            flops=2 * rows * width * (attn_in_weight.size + ffn_in_weight.size) // width,
            bytes_accessed=2 * sum(array.size for array in weights + caches),
            transcendentals=0,
        ),
    )(lengths, tokens, freq, *weights, *caches)


def fits_fused(mesh):
    seq_count, head_count = mesh.shape["seq"], mesh.shape["head"]
    return REQUESTS == 2 * seq_count and D % (128 * seq_count) == 0 and D % (256 * head_count) == 0


def solution(mesh):
    in_specs = (
        P(None, None, "seq"),
        P(None, "seq", "head"),
        P("head", "seq"),
        P(None, "seq", "head"),
        P("head", "seq"),
        P(None, "seq", "head"),
        P(None, "seq", "head"),
        P(),
    )
    out_specs = (P(None, None, "seq"), P(None, None, "seq"))
    body = per_device
    if fits_fused(mesh):
        body = functools.partial(
            fused_device, seq_count=mesh.shape["seq"], head_count=mesh.shape["head"]
        )
    return jax.shard_map(
        body, mesh=mesh, in_specs=in_specs, out_specs=out_specs, check_vma=False
    )
```

```python
import functools

import jax
import jax.numpy as jnp
import numpy as np
from jax import lax
from jax.experimental import pallas as pl
from jax.experimental.pallas import tpu as pltpu
from jax.sharding import PartitionSpec as P

D = 2048
HD = 128
REQUESTS = 16


NORM_EPSILON = 1e-05
NEG_FILL = -1e30


def norm_rows(values):
    center = lax.psum(jnp.sum(values, axis=-1), "seq") / D
    deviate = values - center[:, None]
    spread = lax.psum(jnp.sum(deviate * deviate, axis=-1), "seq") / D
    return deviate * lax.rsqrt(spread + NORM_EPSILON)[:, None]


def rotate_pairs(values, positions):
    half_dim = values.shape[-1] // 2
    inverse_freq = 10000.0 ** (-2.0 * jnp.arange(half_dim, dtype=jnp.float32) / values.shape[-1])
    angles = positions.astype(jnp.float32)[:, None, None] * inverse_freq[None, None, :]
    cosine = jnp.cos(angles)
    sine = jnp.sin(angles)
    first_half = values[..., :half_dim]
    second_half = values[..., half_dim:]
    return jnp.concatenate(
        [first_half * cosine - second_half * sine, second_half * cosine + first_half * sine],
        axis=-1,
    )


def combine_parts(earlier, later_part):
    top_one, total_one, acc_one = earlier
    top_two, total_two, acc_two = later_part
    overall = jnp.maximum(top_one, top_two)
    factor_one = jnp.exp(top_one - overall)
    factor_two = jnp.exp(top_two - overall)
    return (
        overall,
        factor_one * total_one + factor_two * total_two,
        factor_one[..., None] * acc_one + factor_two[..., None] * acc_two,
    )


def per_device(
    tokens,
    attn_in_weight,
    attn_out_weight,
    ffn_in_weight,
    ffn_out_weight,
    cache_keys,
    cache_values,
    lengths,
):
    step_count, request_count, width_local = tokens.shape
    row_count = step_count * request_count
    inputs = tokens.reshape(row_count, width_local).astype(jnp.float32)
    normed = norm_rows(inputs).astype(jnp.bfloat16)
    partial_qkv = jnp.einsum(
        "nd,kde->kne", normed, attn_in_weight, preferred_element_type=jnp.float32
    )
    projected = lax.psum(partial_qkv, "seq")
    heads_local = attn_in_weight.shape[2] // HD
    positions = (lengths[None, :] + jnp.arange(step_count, dtype=jnp.int32)[:, None]).reshape(
        row_count
    )
    query = rotate_pairs(projected[0].reshape(row_count, heads_local, HD), positions).astype(
        jnp.bfloat16
    )
    new_keys = rotate_pairs(projected[1].reshape(row_count, heads_local, HD), positions).astype(
        jnp.bfloat16
    )
    new_values = projected[2].reshape(row_count, heads_local, HD).astype(jnp.bfloat16)
    query = query.reshape(step_count, request_count, heads_local, HD)
    new_keys = new_keys.reshape(step_count, request_count, heads_local, HD)
    new_values = new_values.reshape(step_count, request_count, heads_local, HD)
    score_scale = 1.0 / HD**0.5
    block_len = cache_keys.shape[1]
    key_block = cache_keys.reshape(request_count, block_len, heads_local, HD)
    value_block = cache_values.reshape(request_count, block_len, heads_local, HD)
    first_pos = lax.axis_index("seq") * block_len
    scores = (
        jnp.einsum("trhd,rchd->rthc", query, key_block, preferred_element_type=jnp.float32)
        * score_scale
    )
    places = first_pos + jnp.arange(block_len, dtype=jnp.int32)
    valid = (places[None, :] < lengths[:, None])[:, None, None, :]
    block_top = jnp.max(jnp.where(valid, scores, NEG_FILL), axis=-1)
    weights = jnp.where(valid, jnp.exp(scores - block_top[..., None]), 0.0)
    block_total = jnp.sum(weights, axis=-1)
    block_acc = jnp.einsum(
        "rthc,rchd->rthd",
        weights.astype(jnp.bfloat16),
        value_block,
        preferred_element_type=jnp.float32,
    )
    cache_top = lax.pmax(block_top, "seq")
    rescale = jnp.exp(block_top - cache_top)
    cache_total, cache_acc = lax.psum(
        (rescale * block_total, rescale[..., None] * block_acc), "seq"
    )
    new_scores = (
        jnp.einsum("trhd,urhd->rthu", query, new_keys, preferred_element_type=jnp.float32)
        * score_scale
    )
    causal = (jnp.arange(step_count)[:, None] >= jnp.arange(step_count)[None, :])[None, :, None, :]
    new_top = jnp.max(jnp.where(causal, new_scores, NEG_FILL), axis=-1)
    new_weights = jnp.where(causal, jnp.exp(new_scores - new_top[..., None]), 0.0)
    new_total = jnp.sum(new_weights, axis=-1)
    new_acc = jnp.einsum(
        "rthu,urhd->rthd",
        new_weights.astype(jnp.bfloat16),
        new_values,
        preferred_element_type=jnp.float32,
    )
    overall, denom, numer = combine_parts(
        (cache_top, cache_total, cache_acc), (new_top, new_total, new_acc)
    )
    attended = (
        (numer / denom[..., None])
        .transpose(1, 0, 2, 3)
        .reshape(row_count, heads_local * HD)
        .astype(jnp.bfloat16)
    )
    branch = lax.psum(
        jnp.dot(attended, attn_out_weight, preferred_element_type=jnp.float32), "head"
    )
    resid = inputs + branch
    normed_two = norm_rows(resid).astype(jnp.bfloat16)
    both = lax.psum(
        jnp.einsum("nd,kdf->knf", normed_two, ffn_in_weight, preferred_element_type=jnp.float32),
        "seq",
    )
    hidden = (jax.nn.silu(both[0]) * both[1]).astype(jnp.bfloat16)
    mlp_out = lax.psum(jnp.dot(hidden, ffn_out_weight, preferred_element_type=jnp.float32), "head")
    attn_branch = branch.astype(jnp.bfloat16).reshape(step_count, request_count, width_local)
    mlp_branch = mlp_out.astype(jnp.bfloat16).reshape(step_count, request_count, width_local)
    return (attn_branch, mlp_branch)


MESH = pl.DeviceIdType.MESH
(
    STATS, QKV, QUERY, CACHE, ATTENDED, BRANCH, STATS_TWO, GATE_UP, HIDDEN, DOWN,
    COLUMN_SUM, GATE_UP_PAIR, HIDDEN_PAIR,
) = range(13)
PHASES = 13
PAIR = 2


def to_row(column, eye):
    return jnp.sum(jnp.where(eye, column, 0.0), axis=0, keepdims=True)


def to_column(row, eye):
    return jnp.sum(jnp.where(eye, row, 0.0), axis=1, keepdims=True)


def layer_kernel(
    seq_count,
    head_count,
    lengths_ref,
    tokens_ref,
    freq_ref,
    win_any,
    wout_hbm,
    wffn_hbm,
    wdown_hbm,
    keys_hbm,
    values_hbm,
    attn_out_ref,
    mlp_out_ref,
    win,
    wout,
    wffn,
    wdown,
    keys,
    values,
    stats_buf,
    stats_two_buf,
    qkv_src,
    qkv_buf,
    query_buf,
    cache_src,
    cache_buf,
    attended_buf,
    branch_buf,
    column_src,
    column_buf,
    pair_src,
    pair_buf,
    line_src,
    line_buf,
    hidden_buf,
    down_buf,
    load_sem,
    keys_sem,
    values_sem,
    send_sem,
    recv_sem,
):
    me = lax.axis_index("seq")
    head_me = lax.axis_index("head")
    peers = [lax.rem(me + step, seq_count) for step in range(seq_count)]
    head_peers = [lax.rem(head_me + step, head_count) for step in range(head_count)]
    steps, requests, width = tokens_ref.shape
    rows = steps * requests
    block_len = keys.shape[1]
    cols = keys.shape[2]
    heads = cols // HD
    total_width = width * seq_count

    weight_loads = [
        pltpu.make_async_copy(source, target, load_sem.at[index])
        for index, (source, target) in enumerate(
            [(win_any, win), (wout_hbm, wout), (wffn_hbm, wffn), (wdown_hbm, wdown)]
        )
    ]

    def cache_load(hbm, vmem, sem, index):
        part = pl.ds(2 * index, 2)
        return pltpu.make_async_copy(hbm.at[part], vmem.at[part], sem.at[index])

    weight_loads[0].start()
    for peer in peers:
        cache_load(keys_hbm, keys, keys_sem, peer).start()
        cache_load(values_hbm, values, values_sem, peer).start()
    for load in weight_loads[1:]:
        load.start()

    barrier = pltpu.get_barrier_semaphore()
    for peer in peers[1:]:
        pl.semaphore_signal(barrier, inc=1, device_id={"seq": peer}, device_id_type=MESH)
    for peer in head_peers[1:]:
        pl.semaphore_signal(barrier, inc=1, device_id={"head": peer}, device_id_type=MESH)
    pl.semaphore_wait(barrier, seq_count + head_count - 2)

    sent = []

    def push(source, target, send_slot, recv_slot, peer):
        copy = pltpu.make_async_remote_copy(
            src_ref=source,
            dst_ref=target,
            send_sem=send_sem.at[send_slot[0], send_slot[1]],
            recv_sem=recv_sem.at[recv_slot[0], recv_slot[1]],
            device_id={"seq": peer},
            device_id_type=MESH,
        )
        copy.start()
        sent.append(copy)

    def landed(buf, recv_slot):
        pltpu.make_async_remote_copy(
            src_ref=buf,
            dst_ref=buf,
            send_sem=send_sem.at[recv_slot[0], 0],
            recv_sem=recv_sem.at[recv_slot[0], recv_slot[1]],
            device_id={"seq": peers[1]},
            device_id_type=MESH,
        ).wait_recv()

    def send(phase, step, source, target_buf):
        copy = pltpu.make_async_remote_copy(
            src_ref=source,
            dst_ref=target_buf.at[me],
            send_sem=send_sem.at[phase, step],
            recv_sem=recv_sem.at[phase, me],
            device_id={"seq": peers[step]},
            device_id_type=MESH,
        )
        copy.start()
        sent.append(copy)

    def arrive(phase, step, buf):
        source = lax.rem(me + seq_count - step, seq_count)
        pltpu.make_async_remote_copy(
            src_ref=buf.at[source],
            dst_ref=buf.at[source],
            send_sem=send_sem.at[phase, step],
            recv_sem=recv_sem.at[phase, source],
            device_id={"seq": peers[step]},
            device_id_type=MESH,
        ).wait_recv()
        return source

    def sum_over_heads(phase, buf, partial):
        buf[0] = partial.astype(jnp.bfloat16)
        copies = []
        for step in range(1, head_count):
            copy = pltpu.make_async_remote_copy(
                src_ref=buf.at[0],
                dst_ref=buf.at[step],
                send_sem=send_sem.at[phase, step],
                recv_sem=recv_sem.at[phase, step],
                device_id={"head": head_peers[step]},
                device_id_type=MESH,
            )
            copy.start()
            copies.append(copy)
        sent.extend(copies)
        for copy in copies:
            copy.wait_recv()
        total = jnp.zeros(partial.shape, jnp.float32)
        for device in range(head_count):
            slot = lax.rem(head_me + head_count - device, head_count)
            total = total + buf[slot].astype(jnp.float32)
        return total

    row_iota = lax.broadcasted_iota(jnp.int32, (rows, 128), 0)
    lane_iota = lax.broadcasted_iota(jnp.int32, (rows, 128), 1)
    eye = row_iota == lane_iota
    eye128 = lax.broadcasted_iota(jnp.int32, (128, 128), 0) == lax.broadcasted_iota(
        jnp.int32, (128, 128), 1
    )
    sub8 = lax.broadcasted_iota(jnp.int32, (8, 128), 0)
    lane8 = lax.broadcasted_iota(jnp.int32, (8, 128), 1)

    def send_stats(values_in, phase, buf):
        center = jnp.mean(values_in, axis=1, keepdims=True)
        deviate = values_in - center
        spread = jnp.sum(deviate * deviate, axis=1, keepdims=True)
        buf[me] = jnp.where(
            sub8 == 0, to_row(center, eye), jnp.where(sub8 == 1, to_row(spread, eye), 0.0)
        )
        for step in range(1, seq_count):
            send(phase, step, buf.at[me], buf)
        return deviate

    def join_stats(phase, buf):
        for step in range(1, seq_count):
            arrive(phase, step, buf)
        slots = [buf[index] for index in range(seq_count)]
        mean = sum(slot[0:1] for slot in slots) / seq_count
        offsets = [slot[0:1] - mean for slot in slots]
        square = sum(
            slot[1:2] + width * (offset * offset) for slot, offset in zip(slots, offsets)
        )
        return mean, offsets, lax.rsqrt(square / total_width + NORM_EPSILON)

    perm_row = lax.broadcasted_iota(jnp.int32, (rows, rows), 0)
    perm_col = lax.broadcasted_iota(jnp.int32, (rows, rows), 1)
    to_request_major = (
        (perm_row % steps) * requests + perm_row // steps == perm_col
    ).astype(jnp.bfloat16)
    to_step_major = (
        (perm_col % steps) * requests + perm_col // steps == perm_row
    ).astype(jnp.bfloat16)
    inputs = jnp.dot(
        to_request_major,
        tokens_ref[...].reshape(rows, width),
        preferred_element_type=jnp.float32,
    )
    send_stats(inputs, STATS, stats_buf)
    mean, _, scale = join_stats(STATS, stats_buf)
    normed = ((inputs - to_column(mean, eye)) * to_column(scale, eye)).astype(jnp.bfloat16)

    weight_loads[0].wait()
    parts = [
        jnp.dot(normed, win[index], preferred_element_type=jnp.float32) for index in range(3)
    ]
    joined = jnp.concatenate(parts, axis=1)
    half = joined.shape[1] // 2
    for index in range(seq_count):
        piece = joined[8 * index : 8 * index + 8]
        qkv_src[index] = jnp.concatenate([piece[:, :half], piece[:, half:]], axis=0).astype(
            jnp.bfloat16
        )
    for step in range(1, seq_count):
        send(QKV, step, qkv_src.at[peers[step]], qkv_buf)
    qkv_buf[me] = qkv_src[me]

    request_of = sub8 // steps
    length_rows = jnp.where(request_of == 0, lengths_ref[2 * me], lengths_ref[2 * me + 1])
    position = (length_rows + sub8 % steps).astype(jnp.float32)
    angles = position * freq_ref[...]
    cosine = jnp.cos(angles)
    sine = jnp.sin(angles)
    sine = jnp.where(lane8 < HD // 2, -sine, sine)

    for step in range(1, seq_count):
        arrive(QKV, step, qkv_buf)
    summed = sum(qkv_buf[index].astype(jnp.float32) for index in range(seq_count))
    projected = jnp.concatenate([summed[:8], summed[8:]], axis=1)

    def rotate(block):
        out = []
        for head in range(heads):
            piece = block[:, head * HD : (head + 1) * HD]
            out.append(piece * cosine + pltpu.roll(piece, HD // 2, 1) * sine)
        return jnp.concatenate(out, axis=1)

    query = rotate(projected[:, :cols])
    query_buf[me] = jnp.concatenate(
        [query[:, : cols // 2], query[:, cols // 2 :]], axis=0
    ).astype(jnp.bfloat16)
    for step in range(1, seq_count):
        send(QUERY, step, query_buf.at[me], query_buf)
    new_key = rotate(projected[:, cols : 2 * cols])
    new_value = projected[:, 2 * cols :]

    part = wffn.shape[2] // seq_count
    weight_loads[2].wait()
    ones = jnp.ones((16, width), jnp.bfloat16)
    column_sums = [
        jnp.dot(ones, wffn[index], preferred_element_type=jnp.float32)[:8] for index in range(2)
    ]
    pieces = part // 128
    for index in range(seq_count):
        packed = jnp.zeros((8, 128), jnp.float32)
        for piece in range(2 * pieces):
            start = index * part + (piece % pieces) * 128
            packed = jnp.where(
                sub8 == piece, column_sums[piece // pieces][:, start : start + 128], packed
            )
        column_src[index] = packed
    column_buf[me] = column_src[me]
    for step in range(1, seq_count):
        send(COLUMN_SUM, step, column_src.at[peers[step]], column_buf)

    score_scale = 1.0 / HD**0.5
    lane_head = lax.broadcasted_iota(jnp.int32, (8, cols), 1) // HD
    acc_row = lax.broadcasted_iota(jnp.int32, (8 * heads, cols), 0) % 8

    def spread_heads(block):
        return jnp.concatenate(
            [jnp.where(lane_head == head, block, 0.0) for head in range(heads)], axis=0
        ).astype(jnp.bfloat16)

    def unpack_query(index):
        packed = query_buf[index].astype(jnp.float32)
        return spread_heads(jnp.concatenate([packed[:8], packed[8:]], axis=1))

    def collect(top, total, acc):
        gathered = jnp.zeros((8, cols), jnp.float32)
        stats = jnp.zeros((8, 128), jnp.float32)
        for head in range(heads):
            piece = slice(8 * head, 8 * head + 8)
            gathered = jnp.where(lane_head == head, acc[piece], gathered)
            stats = jnp.where(lane8 == head, top[piece], stats)
            stats = jnp.where(lane8 == 64 + head, total[piece], stats)
        return gathered, stats

    contract_last = (((1,), (1,)), ((), ()))

    chunk = 8 * heads
    together = 128 // chunk
    score_col = lax.broadcasted_iota(jnp.int32, (cols, 128), 1)
    place_col = lax.broadcasted_iota(jnp.int32, (block_len, 128), 1)
    places = lax.broadcasted_iota(jnp.int32, (block_len, 128), 0) + me * block_len

    def cache_blocks(indices):
        wide = jnp.concatenate([unpack_query(index) for index in indices], axis=0)
        wide = wide.astype(jnp.float32).T
        scores = jnp.zeros((block_len, 128), jnp.float32)
        limit = jnp.zeros((block_len, 128), jnp.int32)
        for spot, index in enumerate(indices):
            cache_load(keys_hbm, keys, keys_sem, index).wait()
            for j in range(2):
                mine = (score_col // chunk == spot) & (score_col % 8 // steps == j)
                scores = scores + jnp.dot(
                    keys[2 * index + j],
                    jnp.where(mine, wide, 0.0).astype(jnp.bfloat16),
                    preferred_element_type=jnp.float32,
                )
                mine = (place_col // chunk == spot) & (place_col % 8 // steps == j)
                limit = jnp.where(mine, lengths_ref[2 * index + j], limit)
        scores = scores * score_scale
        valid = places < limit
        top = jnp.max(jnp.where(valid, scores, NEG_FILL), axis=0, keepdims=True)
        weights = jnp.where(valid, jnp.exp(scores - top), 0.0)
        total = jnp.sum(weights, axis=0, keepdims=True)
        top = to_column(top, eye128)
        total = to_column(total, eye128)
        weights = weights.T.astype(jnp.bfloat16)
        out = []
        for spot, index in enumerate(indices):
            cache_load(values_hbm, values, values_sem, index).wait()
            here = slice(spot * chunk, (spot + 1) * chunk)
            accs = [
                jnp.dot(weights[here], values[2 * index + j], preferred_element_type=jnp.float32)
                for j in range(2)
            ]
            out.append(
                collect(top[here], total[here], jnp.where(acc_row < steps, accs[0], accs[1]))
            )
        return out

    for step in range(1, seq_count):
        arrive(QUERY, step, query_buf)
    cache_order = list(range(1, seq_count)) + [0]
    for first in range(0, seq_count, together):
        group = cache_order[first : first + together]
        for step, (gathered, stats) in zip(group, cache_blocks([peers[step] for step in group])):
            target = cache_src.at[peers[step]] if step else cache_buf.at[me]
            target[:, :cols] = gathered
            target[:, cols:] = stats
            if step:
                send(CACHE, step, target, cache_buf)

    own_query = unpack_query(me)
    pad = jnp.zeros((120, cols), jnp.float32)
    wide_key = jnp.concatenate([new_key, pad], axis=0).astype(jnp.bfloat16)
    wide_value = jnp.concatenate([new_value, pad], axis=0).astype(jnp.bfloat16)
    new_scores = (
        lax.dot_general(own_query, wide_key, contract_last, preferred_element_type=jnp.float32)
        * score_scale
    )
    new_row = lax.broadcasted_iota(jnp.int32, new_scores.shape, 0) % 8
    new_col = lax.broadcasted_iota(jnp.int32, new_scores.shape, 1)
    causal = (
        (new_col < 8)
        & (new_col // steps == new_row // steps)
        & (new_col % steps <= new_row % steps)
    )
    new_top = jnp.max(jnp.where(causal, new_scores, NEG_FILL), axis=1, keepdims=True)
    new_weights = jnp.where(causal, jnp.exp(new_scores - new_top), 0.0)
    new_total = jnp.sum(new_weights, axis=1, keepdims=True)
    new_acc = jnp.dot(
        new_weights.astype(jnp.bfloat16), wide_value, preferred_element_type=jnp.float32
    )
    blocks = [collect(new_top, new_total, new_acc)]

    for step in range(1, seq_count):
        arrive(CACHE, step, cache_buf)
    for index in range(seq_count):
        blocks.append((cache_buf[index, :, :cols], cache_buf[index, :, cols:]))
    overall = blocks[0][1]
    for _, stats in blocks[1:]:
        overall = jnp.maximum(overall, stats)
    denom = jnp.zeros((8, 128), jnp.float32)
    numer = jnp.zeros((8, cols), jnp.float32)

    def over_lanes(block):
        return jnp.concatenate(
            [jnp.broadcast_to(block[:, head : head + 1], (8, HD)) for head in range(heads)],
            axis=1,
        )

    for acc, stats in blocks:
        factor = jnp.exp(stats - overall)
        denom = denom + factor * pltpu.roll(stats, 64, 1)
        numer = numer + over_lanes(factor) * acc
    attended = numer / over_lanes(denom)
    attended_buf[me] = jnp.concatenate(
        [attended[:, : cols // 2], attended[:, cols // 2 :]], axis=0
    ).astype(jnp.bfloat16)
    for step in range(1, seq_count):
        send(ATTENDED, step, attended_buf.at[me], attended_buf)
    weight_loads[1].wait()
    for step in range(1, seq_count):
        arrive(ATTENDED, step, attended_buf)
    packed = attended_buf[...].reshape(seq_count * 16, cols // 2)
    upper = jnp.dot(packed, wout[: cols // 2], preferred_element_type=jnp.float32)
    lower = jnp.dot(packed, wout[cols // 2 :], preferred_element_type=jnp.float32)
    partial = (
        upper.reshape(seq_count, 16, width)[:, :8] + lower.reshape(seq_count, 16, width)[:, 8:]
    ).reshape(rows, width)
    branch = sum_over_heads(BRANCH, branch_buf, partial)

    def put_out(ref, value):
        ref[...] = (
            jnp.dot(to_step_major, value.astype(jnp.bfloat16), preferred_element_type=jnp.float32)
            .astype(jnp.bfloat16)
            .reshape(ref.shape)
        )

    put_out(attn_out_ref, branch)
    lines = seq_count // PAIR
    line, place_in_pair = me // PAIR, me % PAIR
    partner = line * PAIR + (PAIR - 1 - place_in_pair)
    line_peers = [lax.rem(line + step, lines) * PAIR + place_in_pair for step in range(lines)]
    across = [lax.rem(line + step, lines) * PAIR + (PAIR - 1 - place_in_pair) for step in range(lines)]
    centred = send_stats(inputs + branch, STATS_TWO, stats_two_buf).astype(jnp.bfloat16)

    def gate_up(index):
        place = pl.ds(pl.multiple_of(index * part, part), part)
        return jnp.concatenate(
            [
                jnp.dot(centred, wffn[which, :, place], preferred_element_type=jnp.float32)
                for which in range(2)
            ],
            axis=1,
        )

    order = list(range(1, lines)) + [0]
    for step in order:
        pair_src[step] = gate_up(across[step]).astype(jnp.bfloat16)
        push(
            pair_src.at[step], pair_buf.at[step], (GATE_UP_PAIR, step), (GATE_UP_PAIR, step), partner
        )
    for step in order:
        own = gate_up(line_peers[step])
        landed(pair_buf.at[step], (GATE_UP_PAIR, step))
        both = own + pair_buf[step].astype(jnp.float32)
        if step:
            line_src[step] = both.astype(jnp.bfloat16)
            push(
                line_src.at[step],
                line_buf.at[step],
                (GATE_UP, step),
                (GATE_UP, step),
                line_peers[step],
            )
    _, offsets, scale = join_stats(STATS_TWO, stats_two_buf)
    for step in range(1, seq_count):
        arrive(COLUMN_SUM, step, column_buf)
    for index in range(seq_count):
        sums = column_buf[index]
        sums = jnp.concatenate([sums[j : j + 1] for j in range(2 * pieces)], axis=1)
        both = both + to_column(offsets[index], eye) * sums
    scale = to_column(scale, eye)
    for step in range(1, lines):
        landed(line_buf.at[step], (GATE_UP, step))
        both = both + line_buf[step].astype(jnp.float32)
    both = both * scale
    gate = both[:, :part]
    hidden_buf[me] = (gate / (1.0 + jnp.exp(-gate)) * both[:, part:]).astype(jnp.bfloat16)

    def share(index, step):
        push(
            hidden_buf.at[index], hidden_buf.at[index], (HIDDEN_PAIR, step), (HIDDEN, index), partner
        )

    def down(index):
        place = pl.ds(pl.multiple_of(index * part, part), part)
        return jnp.dot(hidden_buf[index], wdown[place, :], preferred_element_type=jnp.float32)

    for step in range(1, lines):
        push(hidden_buf.at[me], hidden_buf.at[me], (HIDDEN, step), (HIDDEN, me), line_peers[step])
    share(me, 0)
    weight_loads[3].wait()
    partial = down(me)
    for step in range(1, lines):
        landed(hidden_buf.at[line_peers[step]], (HIDDEN, line_peers[step]))
        share(line_peers[step], step)
        partial = partial + down(line_peers[step])
    for step in range(lines):
        landed(hidden_buf.at[across[step]], (HIDDEN, across[step]))
        partial = partial + down(across[step])
    put_out(mlp_out_ref, sum_over_heads(DOWN, down_buf, partial))
    for copy in sent:
        copy.wait_send()


def fused_device(
    tokens,
    attn_in_weight,
    attn_out_weight,
    ffn_in_weight,
    ffn_out_weight,
    cache_keys,
    cache_values,
    lengths,
    *,
    seq_count,
    head_count,
):
    rows = tokens.shape[0] * tokens.shape[1]
    width = tokens.shape[2]
    cols = cache_keys.shape[2]
    part = ffn_in_weight.shape[2] // seq_count
    inverse_freq = 10000.0 ** (-2.0 * np.arange(HD // 2) / HD)
    freq = jnp.asarray(np.tile(inverse_freq, 2)[None, :].astype(np.float32))
    bf16, f32 = jnp.bfloat16, jnp.float32
    in_vmem = pl.BlockSpec(memory_space=pltpu.VMEM)
    in_any = pl.BlockSpec(memory_space=pl.ANY)
    weights = (attn_in_weight, attn_out_weight, ffn_in_weight, ffn_out_weight)
    caches = (cache_keys, cache_values)
    return pl.pallas_call(
        functools.partial(layer_kernel, seq_count, head_count),
        out_shape=[jax.ShapeDtypeStruct(tokens.shape, bf16)] * 2,
        in_specs=[pl.BlockSpec(memory_space=pltpu.SMEM), in_vmem, in_vmem] + [in_any] * 6,
        out_specs=[in_vmem] * 2,
        scratch_shapes=[pltpu.VMEM(array.shape, bf16) for array in weights + caches]
        + [
            pltpu.VMEM((seq_count, 8, 128), f32),
            pltpu.VMEM((seq_count, 8, 128), f32),
            pltpu.VMEM((seq_count, 16, 3 * cols // 2), bf16),
            pltpu.VMEM((seq_count, 16, 3 * cols // 2), bf16),
            pltpu.VMEM((seq_count, 16, cols // 2), bf16),
            pltpu.VMEM((seq_count, 8, cols + 128), f32),
            pltpu.VMEM((seq_count, 8, cols + 128), f32),
            pltpu.VMEM((seq_count, 16, cols // 2), bf16),
            pltpu.VMEM((head_count, rows, width), bf16),
            pltpu.VMEM((seq_count, 8, 128), f32),
            pltpu.VMEM((seq_count, 8, 128), f32),
            pltpu.VMEM((seq_count // PAIR, rows, 2 * part), bf16),
            pltpu.VMEM((seq_count // PAIR, rows, 2 * part), bf16),
            pltpu.VMEM((seq_count // PAIR, rows, 2 * part), bf16),
            pltpu.VMEM((seq_count // PAIR, rows, 2 * part), bf16),
            pltpu.VMEM((seq_count, rows, part), bf16),
            pltpu.VMEM((head_count, rows, width), bf16),
            pltpu.SemaphoreType.DMA((4,)),
            pltpu.SemaphoreType.DMA((seq_count,)),
            pltpu.SemaphoreType.DMA((seq_count,)),
            pltpu.SemaphoreType.DMA((PHASES, max(seq_count, head_count))),
            pltpu.SemaphoreType.DMA((PHASES, max(seq_count, head_count))),
        ],
        compiler_params=pltpu.CompilerParams(
            collective_id=0, has_side_effects=True, vmem_limit_bytes=60 * 2**20
        ),
        cost_estimate=pl.CostEstimate(
            flops=2 * rows * width * (attn_in_weight.size + ffn_in_weight.size) // width,
            bytes_accessed=2 * sum(array.size for array in weights + caches),
            transcendentals=0,
        ),
    )(lengths, tokens, freq, *weights, *caches)


def fits_fused(mesh):
    seq_count, head_count = mesh.shape["seq"], mesh.shape["head"]
    return REQUESTS == 2 * seq_count and D % (128 * seq_count) == 0 and D % (256 * head_count) == 0


def solution(mesh):
    in_specs = (
        P(None, None, "seq"),
        P(None, "seq", "head"),
        P("head", "seq"),
        P(None, "seq", "head"),
        P("head", "seq"),
        P(None, "seq", "head"),
        P(None, "seq", "head"),
        P(),
    )
    out_specs = (P(None, None, "seq"), P(None, None, "seq"))
    body = per_device
    if fits_fused(mesh):
        body = functools.partial(
            fused_device, seq_count=mesh.shape["seq"], head_count=mesh.shape["head"]
        )
    return jax.shard_map(
        body, mesh=mesh, in_specs=in_specs, out_specs=out_specs, check_vma=False
    )
```
